32 devices in a mesh: member: 4 (over y, core), tile: 8 (over z, x).
Axes of the slice: x: 2, y: 2, z: 4, core: 2. Of those that a mesh axis runs over, the one named last changes fastest.
Arguments:
- perturb: bfloat16 [64, 128, 2560], P('member', 'tile'), may hold values from -0.75 to 0.75
- weights: float32 [64, 32, 1280], P('member', 'tile'), may hold values from -1.2 to 1.2
- column_map: bfloat16 [1280, 2560], replicated, may hold values from -0.15625 to 0.15625
- background: float32 [128, 2560], P('tile', 'member'), may hold values from -6 to 6
- stencil_index: int32 [8, 32, 4, 8], P('tile'), may hold values from 0 to 9598, as said below
- row_fraction: float32 [8, 32, 4, 8], P('tile'), may hold values from 0 to 1
- column_fraction: float32 [8, 32, 4, 8], P('tile'), may hold values from 0 to 1
- block_lengths: int32 [8, 32, 4], P('tile'), may hold values from 0 to 8, as said below
- obs_value: float32 [32, 32, 8], P(('member', 'tile')), may hold values from -6 to 6
- obs_error: float32 [32, 32, 8], P(('member', 'tile')), may hold values from 0.3 to 1
- instrument_gain: float32 [32], P(('member', 'tile')), may hold values from 0.2 to 0.8
Outputs:
- analysis_weights: float32 [64, 32, 1280], P('member', 'tile')
- analysis_increment: float32 [128, 2560], P('tile', 'member')
The draws below stay inside these ranges and needn't reach their ends.
Inputs may be any that keep to these rules, and one draw needn't show every extreme that they name: stencil_index = r * 640 + c with 0 <= r < 15 and 0 <= c < 639. `block_lengths`: in every draw some owner (one tile and one member index) has all its blocks full.
All inputs are finite; a program needn't handle non-finite values.
Results may differ from the reference program's by a relative error of at most 0.0022.
Values may be sent and summed in bfloat16 or wider, within the bound.
A program may use at most 64 MiB of HBM per device.

```python
import math
import jax
import jax.numpy as jnp
from jax import lax

RATIO = 4
KSM = 3
ITERS = 1
CC = 1280
FC = 2560
MEM_DEV = 16
CAP = 8
MEMBERS = 64
TILES = 8
GROUPS = 4
NCR = 32
FR = 16
NFR = 128
CW = 640
N_MEMBER = 4
N_TILE = 8
DEVICES = 32


def draw_stencil_index(key, part):
    array_shape = (TILES, DEVICES, GROUPS, CAP)
    first_key, second_key = jax.random.split(key)
    row_pick = jax.random.randint(first_key, array_shape, 0, FR - 1)
    column_pick = jax.random.randint(second_key, array_shape, 0, CW - 1)
    return (row_pick * CW + column_pick).astype(jnp.int32)


def draw_block_lengths(key, part):
    first_key, second_key, third_key, fourth_key = jax.random.split(key, 4)
    base_counts = jax.random.randint(first_key, (TILES, DEVICES, GROUPS), 0, CAP // 2 + 1)
    busy_owner = jax.random.randint(second_key, (TILES, 1, GROUPS), 0, 8) == 0
    chosen_tile = jax.random.randint(third_key, (), 0, TILES)
    chosen_group = jax.random.randint(fourth_key, (), 0, GROUPS)
    tile_ids = lax.broadcasted_iota(jnp.int32, (TILES, 1, GROUPS), 0)
    group_ids = lax.broadcasted_iota(jnp.int32, (TILES, 1, GROUPS), 2)
    forced = (tile_ids == chosen_tile) & (group_ids == chosen_group)
    return jnp.where(busy_owner | forced, CAP, base_counts).astype(jnp.int32)


def shard_levels(stream_key, shape, cuts, least, high):
    loudness, own = 1.0, jax.random.fold_in(stream_key, 6)
    for axis_at, parts in cuts:
        heights = jnp.exp(jax.random.uniform(jax.random.fold_in(own, axis_at), (parts,), jnp.float32, least / len(cuts), high / len(cuts)))
        loudness = loudness * jnp.repeat(heights, shape[axis_at] // parts).reshape([-1 if axis == axis_at else 1 for axis in range(len(shape))])
    return loudness


def scatter_about(key, extent, scale, limit, cuts=(), kind=jnp.bfloat16):
    factor_of = shard_levels(key, extent, cuts, -0.22, 0.18) if cuts else 1.0
    array = jax.random.normal(key, extent, jnp.float32) * scale * factor_of
    return jnp.minimum(jnp.maximum(array, -limit), limit).astype(kind)


def setup_inputs(seed: int = 0) -> dict:
    arg_keys = jax.random.split(jax.random.key(seed), 12)
    perturb = scatter_about(arg_keys[0], (MEMBERS, NFR, FC), MEMBERS ** -0.5, 0.75, ((0, 4), (1, 8)))
    weights = scatter_about(arg_keys[1], (MEMBERS, NCR, CC), 0.2, 1.2, ((0, 4), (1, 8)), jnp.float32)
    column_map = scatter_about(arg_keys[2], (CC, FC), CC ** -0.5, 0.15625)
    background = scatter_about(arg_keys[3], (NFR, FC), 1.0, 6.0, ((0, 8), (1, 4)), jnp.float32)
    stencil_index = draw_stencil_index(jax.random.fold_in(arg_keys[11], 71), 0)
    row_fraction = jnp.clip(1.0 * jax.random.uniform(arg_keys[5], (TILES, DEVICES, GROUPS, CAP), jnp.float32) ** shard_levels(arg_keys[5], (TILES, DEVICES, GROUPS, CAP), ((0, 8),), -0.2, 0.2), 0.0, 1.0)
    column_fraction = jnp.clip(1.0 * jax.random.uniform(arg_keys[6], (TILES, DEVICES, GROUPS, CAP), jnp.float32) ** shard_levels(arg_keys[6], (TILES, DEVICES, GROUPS, CAP), ((0, 8),), -0.2, 0.2), 0.0, 1.0)
    block_lengths = draw_block_lengths(jax.random.fold_in(arg_keys[11], 71), 0)
    obs_value = scatter_about(arg_keys[8], (DEVICES, DEVICES, CAP), 1.0, 6.0, ((0, 32),), jnp.float32)
    obs_error = jnp.clip(jnp.exp(math.log(1.0) - 1.2039728 * jax.random.uniform(arg_keys[9], (DEVICES, DEVICES, CAP), jnp.float32) ** shard_levels(arg_keys[9], (DEVICES, DEVICES, CAP), ((0, 32),), -0.2, 0.2)), 0.3, 1.0)
    instrument_gain = jnp.clip(0.2 + 0.6 * jax.random.uniform(arg_keys[10], (DEVICES,), jnp.float32) ** shard_levels(arg_keys[10], (DEVICES,), ((0, 32),), -0.2, 0.2), 0.2, 0.8)
    return dict(perturb=perturb, weights=weights, column_map=column_map, background=background, stencil_index=stencil_index, row_fraction=row_fraction, column_fraction=column_fraction, block_lengths=block_lengths, obs_value=obs_value, obs_error=obs_error, instrument_gain=instrument_gain)


DIFFUSION = 0.45


def smooth(grid_values):
    for pass_index in range(KSM):
        padded = jnp.pad(grid_values, ((0, 0), (1, 1), (0, 0)))
        grid_values = grid_values + DIFFUSION * (padded[:, :-2] + padded[:, 2:] - 2.0 * grid_values)
    return grid_values


def refine(extended):
    members_here, row_count, col_count = extended.shape
    lower_rows = extended[:, :-2]
    middle = extended[:, 1:-1]
    upper_rows = extended[:, 2:]
    pieces = []
    for offset in range(RATIO):
        shift_value = (offset + 0.5) / RATIO - 0.5
        if shift_value < 0:
            pieces.append((1.0 + shift_value) * middle - shift_value * lower_rows)
        else:
            pieces.append((1.0 - shift_value) * middle + shift_value * upper_rows)
    return jnp.stack(pieces, axis=2).reshape(members_here, (row_count - 2) * RATIO, col_count)


def refine_adjoint(fine_field):
    members_here, fine_count, col_count = fine_field.shape
    row_count = fine_count // RATIO
    blocks = fine_field.reshape(members_here, row_count, RATIO, col_count)
    middle = jnp.zeros_like(blocks[:, :, 0])
    lower_rows = jnp.zeros_like(middle)
    upper_rows = jnp.zeros_like(middle)
    for offset in range(RATIO):
        shift_value = (offset + 0.5) / RATIO - 0.5
        fine_layer = blocks[:, :, offset]
        if shift_value < 0:
            middle = middle + (1.0 + shift_value) * fine_layer
            lower_rows = lower_rows - shift_value * fine_layer
        else:
            middle = middle + (1.0 - shift_value) * fine_layer
            upper_rows = upper_rows + shift_value * fine_layer
    return (jnp.pad(middle, ((0, 0), (1, 1), (0, 0))) + jnp.pad(lower_rows, ((0, 0), (0, 2), (0, 0)))
            + jnp.pad(upper_rows, ((0, 0), (2, 0), (0, 0))))


def forward(coarse, perturb, column_map):
    smoothed_all = smooth(coarse).reshape(N_MEMBER, MEM_DEV, NCR, CC)
    members_grouped = perturb.reshape(N_MEMBER, MEM_DEV, NFR, FC)

    def add_group(accumulated, group_items):
        smoothed_part, perturb_part = group_items
        mapped = jnp.dot(smoothed_part.astype(jnp.bfloat16).reshape(-1, CC), column_map,
                         preferred_element_type=jnp.float32).reshape(MEM_DEV, NCR, FC)
        fine_field = refine(jnp.pad(mapped, ((0, 0), (1, 1), (0, 0))))
        return accumulated + jnp.sum(fine_field * perturb_part.astype(jnp.float32), axis=0), None

    accumulated, unused = lax.scan(add_group, jnp.zeros((NFR, FC), jnp.float32), (smoothed_all, members_grouped))
    return accumulated


def adjoint_map(spread_field, perturb, column_map):
    members_grouped = perturb.reshape(N_MEMBER, MEM_DEV, NFR, FC)

    def one_group(perturb_part):
        edge_terms = refine_adjoint(perturb_part.astype(jnp.float32) * spread_field)
        inner_rows = edge_terms[:, 1:-1].astype(jnp.bfloat16)
        pulled = lax.dot_general(inner_rows.reshape(-1, FC), column_map, (((1,), (1,)), ((), ())),
                                 preferred_element_type=jnp.float32)
        return pulled.reshape(MEM_DEV, NCR, CC)

    pulled_all = lax.map(one_group, members_grouped).reshape(MEMBERS, NCR, CC)
    return smooth(pulled_all)


def global_points(stencil_index):
    tile_ids = lax.broadcasted_iota(jnp.int32, stencil_index.shape, 0)
    group_ids = lax.broadcasted_iota(jnp.int32, stencil_index.shape, 2)
    row_ids = tile_ids * FR + stencil_index // CW
    col_ids = group_ids * CW + stencil_index % CW
    return (row_ids * FC + col_ids).astype(jnp.int32)


def interpolate(field_flat, corner, row_fraction, column_fraction, stride):
    return ((1.0 - row_fraction) * (1.0 - column_fraction) * field_flat[corner]
            + (1.0 - row_fraction) * column_fraction * field_flat[corner + 1]
            + row_fraction * (1.0 - column_fraction) * field_flat[corner + stride]
            + row_fraction * column_fraction * field_flat[corner + stride + 1])


def spread(residual, corner, row_fraction, column_fraction, stride, total_size):
    positions = jnp.concatenate([corner.reshape(-1), (corner + 1).reshape(-1),
                                 (corner + stride).reshape(-1), (corner + stride + 1).reshape(-1)])
    amounts = jnp.concatenate([
        ((1.0 - row_fraction) * (1.0 - column_fraction) * residual).reshape(-1),
        ((1.0 - row_fraction) * column_fraction * residual).reshape(-1),
        (row_fraction * (1.0 - column_fraction) * residual).reshape(-1),
        (row_fraction * column_fraction * residual).reshape(-1)])
    return jnp.zeros((total_size,), jnp.float32).at[positions].add(amounts)


def innovation(obs_state, obs_value, obs_error, instrument):
    bounded = jnp.tanh(obs_state)
    derivative = 1.0 + instrument * (1.0 - bounded * bounded)
    misfit = obs_state + instrument * bounded - obs_value
    precision_obs = 1.0 / (obs_error * obs_error)
    return derivative * misfit * precision_obs, derivative * derivative * precision_obs


def to_owner_layout(values):
    return jnp.transpose(values.reshape(DEVICES, N_MEMBER, N_TILE, CAP), (2, 0, 1, 3))


def reference(perturb, weights, column_map, background, stencil_index, row_fraction, column_fraction,
              block_lengths, obs_value, obs_error, instrument_gain):
    corner = global_points(stencil_index)
    slot_ids = lax.broadcasted_iota(jnp.int32, stencil_index.shape, 3)
    valid_slots = (slot_ids < block_lengths[:, :, :, None]).astype(jnp.float32)
    coarse = weights
    increment = forward(coarse, perturb, column_map)
    obs_state = interpolate((background + increment).reshape(-1), corner, row_fraction, column_fraction, FC)
    for iteration in range(ITERS):
        batch_state = jnp.transpose(obs_state, (1, 2, 0, 3)).reshape(DEVICES, DEVICES, CAP)
        residual, obs_weight = innovation(batch_state, obs_value, obs_error, instrument_gain[:, None, None])
        residual = to_owner_layout(residual) * valid_slots
        obs_weight = to_owner_layout(obs_weight)
        spread_field = spread(residual, corner, row_fraction, column_fraction, FC, NFR * FC).reshape(NFR, FC)
        gradient = coarse + adjoint_map(spread_field, perturb, column_map)
        grad_square = jnp.sum(gradient * gradient)
        grad_image = forward(gradient, perturb, column_map)
        grad_obs = interpolate(grad_image.reshape(-1), corner, row_fraction, column_fraction, FC)
        curvature = jnp.sum(valid_slots * obs_weight * grad_obs * grad_obs)
        step_size = grad_square / (grad_square + curvature)
        coarse = coarse - step_size * gradient
        increment = increment - step_size * grad_image
        obs_state = obs_state - step_size * grad_obs
    return coarse, increment
```

```python
import functools

import jax
import jax.numpy as jnp
from jax import lax
from jax.experimental import pallas as pl
from jax.experimental.pallas import tpu as pltpu
from jax.sharding import PartitionSpec as P

RATIO = 4
KSM = 3
DIFFUSION = 0.45
BLOCK = 256
LANES = 128
MESH = pl.DeviceIdType.MESH
F32 = jnp.float32
BF16 = jnp.bfloat16


def sweep(rows, first, mask_of):
    for _ in range(KSM):
        first += 1
        inner = []
        for at in range(1, len(rows) - 1):
            mid = rows[at]
            new = mid + DIFFUSION * (rows[at - 1] + rows[at + 1] - 2.0 * mid)
            mask = mask_of(first + at - 1)
            inner.append(new if mask is None else new * mask)
        rows = inner
    return rows


def split_rows(values):
    high = values.astype(BF16)
    low = (values - high.astype(F32)).astype(BF16)
    return jnp.concatenate([high, low], axis=0)


def kernel(
    members,
    tiles,
    pay_ref,
    w_ref,
    obs_ref,
    bg_ref,
    map_hbm,
    per_hbm,
    outw_ref,
    outi_ref,
    cmap,
    per,
    hot,
    rowf,
    fields,
    obsin,
    wsend,
    halo,
    acc,
    flat,
    part,
    frecv,
    hsend,
    hrecv,
    ssend,
    srecv,
    spread,
    edges,
    pown,
    psend,
    precv,
    grad,
    load_sem,
    o1_send,
    o1_recv,
    o2_send,
    o2_recv,
    w_send,
    w_recv,
    h_send,
    h_recv,
    f_send,
    f_recv,
    p_send,
    p_recv,
    s_send,
    s_recv,
):
    m = lax.axis_index("member")
    t = lax.axis_index("tile")
    chunks, rows, mem, width = w_ref.shape
    region = bg_ref.shape[1]
    fine_rows = bg_ref.shape[0]
    slots = obs_ref.shape[2]
    fine_cols = cmap.shape[1]
    ext = rows + 2
    cap = slots // (members * tiles)
    scalar_row = hsend.shape[1] - 8

    load_map = pltpu.make_async_copy(map_hbm, cmap, load_sem.at[0])
    load_per = pltpu.make_async_copy(per_hbm, per, load_sem.at[1])
    load_map.start()
    load_per.start()

    barrier = pltpu.get_barrier_semaphore()
    for d in range(1, members):
        pl.semaphore_signal(
            barrier, inc=1, device_id=(lax.rem(m + d, members), t), device_id_type=MESH
        )
    for d in range(1, tiles):
        pl.semaphore_signal(
            barrier, inc=1, device_id=(m, lax.rem(t + d, tiles)), device_id_type=MESH
        )

    wsend[...] = w_ref[...].astype(BF16)
    obsin[m, t] = pay_ref[t]
    pl.semaphore_wait(barrier, members + tiles - 2)

    def remote(src, dst, ssem, rsem, where):
        return pltpu.make_async_remote_copy(
            src_ref=src, dst_ref=dst, send_sem=ssem, recv_sem=rsem, device_id=where, device_id_type=MESH
        )

    def halo_copy(side, j):
        target = jnp.clip(t + 1 - 2 * side, 0, tiles - 1)
        return remote(
            wsend.at[j], halo.at[side, j], w_send.at[side, j], w_recv.at[side, j], (m, target)
        )

    def has_target(step):
        return (t + step >= 0) & (t + step < tiles)

    def first_obs(d):
        to = lax.rem(t + d, tiles)
        return remote(pay_ref.at[to], obsin.at[m, t], o1_send.at[d], o1_recv.at[d], (m, to))

    def second_obs(d):
        to = lax.rem(m + d, members)
        return remote(obsin.at[m], obsin.at[m], o2_send.at[d], o2_recv.at[d], (to, t))

    for d in range(1, tiles):
        first_obs(d).start()

    def send_halo(j, carry):
        for side in range(2):

            @pl.when(has_target(1 - 2 * side))
            def _():
                halo_copy(side, j).start()

        return carry

    lax.fori_loop(0, chunks, send_halo, 0)

    for side in range(2):

        @pl.when(jnp.logical_not(has_target(2 * side - 1)))
        def _():
            halo[side] = jnp.zeros(halo.shape[1:], halo.dtype)

    shifts = (-1, 1, -2, 2)
    for at, shift in enumerate(shifts):

        @pl.when(jnp.logical_not(has_target(shift)))
        def _():
            precv[at] = jnp.zeros(precv.shape[1:], precv.dtype)

    hsend[...] = jnp.zeros(hsend.shape, hsend.dtype)

    def prepare(k, carry):
        info = obs_ref[k]
        row_pos, col_pos, row_frac = info[0:1], info[1:2], info[2:3]
        col_ids = lax.broadcasted_iota(jnp.int32, (region, slots), 0).astype(F32)
        hot[k, :, 0:slots] = jnp.where(col_ids == col_pos, 1.0, 0.0).astype(BF16)
        hot[k, :, slots : 2 * slots] = jnp.where(col_ids == col_pos + 1.0, 1.0, 0.0).astype(BF16)
        row_ids = lax.broadcasted_iota(jnp.int32, (fine_rows, slots), 0).astype(F32)
        rowf[k] = jnp.where(row_ids == row_pos, 1.0 - row_frac, 0.0) + jnp.where(
            row_ids == row_pos + 1.0, row_frac, 0.0
        )
        return carry

    lax.fori_loop(0, members, prepare, 0)

    for d in range(1, tiles):
        first_obs(d).wait_recv()
    for d in range(1, members):
        second_obs(d).start()

    low1 = jnp.where(t > 0, 1.0, 0.0).astype(F32)
    high1 = jnp.where(t < tiles - 1, 1.0, 0.0).astype(F32)
    low2 = jnp.where(t > 1, 1.0, 0.0).astype(F32)
    high2 = jnp.where(t < tiles - 2, 1.0, 0.0).astype(F32)

    def mask_of(row):
        if row < -rows:
            return low2
        if row < 0:
            return low1
        if row < rows:
            return None
        if row < 2 * rows:
            return high1
        return high2

    def extended_weights(j, at):
        cols = pl.ds(at * LANES, LANES)
        return (
            [halo[0, j, r, :, cols].astype(F32) for r in range(rows)]
            + [w_ref[j, r, :, cols] for r in range(rows)]
            + [halo[1, j, r, :, cols].astype(F32) for r in range(rows)]
        )

    def map_chunk(j, lhs):
        depth = pl.ds(pl.multiple_of(j * width, width), width)
        product = jnp.dot(lhs, cmap[depth, :], preferred_element_type=F32)

        @pl.when(j == 0)
        def _():
            acc[...] = product

        @pl.when(j > 0)
        def _():
            acc[...] += product

    def smooth_to_lhs(pieces):
        return jnp.concatenate(
            [
                jnp.concatenate([piece[r] for piece in pieces], axis=1).astype(BF16)
                for r in range(ext)
            ],
            axis=0,
        )

    def first_forward(j, carry):
        for side in range(2):

            @pl.when(has_target(2 * side - 1))
            def _():
                halo_copy(side, j).wait_recv()

        map_chunk(
            j,
            smooth_to_lhs(
                [sweep(extended_weights(j, at), -rows, mask_of) for at in range(width // LANES)]
            ),
        )
        return carry

    load_map.wait()
    load_per.wait()
    lax.fori_loop(0, chunks, first_forward, 0)

    weights_of = []
    for offset in range(RATIO):
        shift = (offset + 0.5) / RATIO - 0.5
        weights_of.append((1.0 - abs(shift), abs(shift), -1 if shift < 0 else 1))

    def member_sum(block, carry):
        cols = pl.ds(pl.multiple_of(block * LANES, LANES), LANES)
        mapped = [acc[pl.ds(i * mem, mem), cols] for i in range(ext)]
        lines = []
        for i in range(rows):
            for offset in range(RATIO):
                near, far, side = weights_of[offset]
                fine = near * mapped[i + 1] + far * mapped[i + 1 + side]
                term = fine * per[RATIO * i + offset, :, cols].astype(F32)
                lines.append(jnp.sum(term, axis=0, keepdims=True))
        flat[:, cols] = jnp.concatenate(lines, axis=0)
        return carry

    def part_copy(which, d):
        to = lax.rem(m + d, members)
        return remote(
            part.at[which, to], frecv.at[which, m], f_send.at[which, d], f_recv.at[which, d], (to, t)
        )

    def h_copy(which, d):
        to = lax.rem(m + d, members)
        return remote(
            hsend.at[which], hrecv.at[which, m], h_send.at[which, d], h_recv.at[which, d], (to, t)
        )

    def observe(which, scale):
        lax.fori_loop(0, fine_cols // LANES, member_sum, 0)
        for k in range(members):
            field = flat[:, k * region : (k + 1) * region]
            part[which, k] = field
            if which == 0:
                field = field + bg_ref[...] * jnp.where(m == k, 1.0, 0.0).astype(F32)
            found = jnp.dot(split_rows(field), hot[k], preferred_element_type=F32)
            found = found[:fine_rows] + found[fine_rows:]
            col_frac = obs_ref[k][3:4]
            along = (1.0 - col_frac) * found[:, :slots] + col_frac * found[:, slots:]
            hsend[which, k : k + 1, :] = jnp.sum(along * rowf[k], axis=0, keepdims=True)
        for d in range(1, members):
            h_copy(which, d).start()
        for d in range(1, members):
            part_copy(which, d).start()

    def gathered(which):
        hrecv[which, m] = hsend[which]
        for d in range(1, members):
            h_copy(which, d).wait_recv()
        total = hrecv[which, 0]
        for k in range(1, members):
            total = total + hrecv[which, k]
        return total

    observe(0, None)

    for d in range(1, members):
        second_obs(d).wait_recv()
    listed = obsin[...].reshape(members * tiles * 8, LANES)
    owner_ids = lax.broadcasted_iota(jnp.int32, (members * tiles, 8, slots), 0)
    lane_ids = lax.broadcasted_iota(jnp.int32, (members * tiles, 8, slots), 2)
    chosen = lane_ids // cap == owner_ids
    source = lax.broadcasted_iota(jnp.int32, (LANES, slots), 0)
    target = lax.broadcasted_iota(jnp.int32, (LANES, slots), 1)
    for k in range(members):
        pick = jnp.where(source == k * cap + target % cap, 1.0, 0.0).astype(F32)
        wide = jnp.dot(listed, pick, precision=lax.Precision.HIGHEST, preferred_element_type=F32)
        wide = wide.reshape(members * tiles, 8, slots)
        fields[k] = jnp.sum(jnp.where(chosen, wide, 0.0), axis=0)

    state = gathered(0)

    for k in range(members):
        value, error, gain = fields[k][0:1], fields[k][1:2], fields[k][2:3]
        here = state[k : k + 1]
        bounded = jnp.tanh(here)
        slope = 1.0 + gain * (1.0 - bounded * bounded)
        precision = 1.0 / (error * error)
        live = obs_ref[k][4:5]
        residual = slope * (here + gain * bounded - value) * precision * live
        fields[k, 3:4] = slope * slope * precision * live
        col_frac = obs_ref[k][3:4]
        weighted = rowf[k] * residual
        both = jnp.concatenate([weighted * (1.0 - col_frac), weighted * col_frac], axis=1)
        found = lax.dot_general(
            split_rows(both), hot[k], (((1,), (1,)), ((), ())), preferred_element_type=F32
        )
        spread[:, k * region : (k + 1) * region] = found[:fine_rows] + found[fine_rows:]

    def adjoint_terms(block, carry):
        cols = pl.ds(pl.multiple_of(block * LANES, LANES), LANES)
        here = spread[:, cols]
        terms = [None] * ext

        def add(at, value):
            terms[at] = value if terms[at] is None else terms[at] + value

        for i in range(rows):
            for offset in range(RATIO):
                near, far, side = weights_of[offset]
                r = RATIO * i + offset
                layer = per[r, :, cols].astype(F32) * here[r : r + 1]
                add(i + 1, near * layer)
                add(i + 1 + side, far * layer)
        for at in range(ext):
            edges[pl.ds(at * mem, mem), cols] = terms[at].astype(BF16)
        return carry

    lax.fori_loop(0, fine_cols // LANES, adjoint_terms, 0)

    spans = {-1: (0, ext), 1: (0, ext), -2: (ext - rows, ext), 2: (0, rows)}

    def pulled_copy(at, j):
        shift = shifts[at]
        begin, end = spans[shift]
        to = jnp.clip(t - shift, 0, tiles - 1)
        return remote(
            psend.at[j, pl.ds(begin, end - begin)],
            precv.at[at, j, pl.ds(begin, end - begin)],
            p_send.at[at, j],
            p_recv.at[at, j],
            (m, to),
        )

    def pull(j, carry):
        depth = pl.ds(pl.multiple_of(j * width, width), width)
        product = lax.dot_general(
            edges[...], cmap[depth, :], (((1,), (1,)), ((), ())), preferred_element_type=F32
        ).reshape(ext, mem, width)
        pown[j] = product
        psend[j] = product.astype(BF16)
        for at, shift in enumerate(shifts):

            @pl.when(has_target(-shift))
            def _():
                pulled_copy(at, j).start()

        return carry

    lax.fori_loop(0, chunks, pull, 0)

    def second_forward(j, square):
        for at, shift in enumerate(shifts):

            @pl.when(has_target(shift))
            def _():
                pulled_copy(at, j).wait_recv()

        pieces = []
        for lane in range(width // LANES):
            cols = pl.ds(lane * LANES, LANES)
            lowest = -rows - KSM
            pulled = [None] * (rows + 2 * (rows + KSM))

            def put(row, value):
                at = row - lowest
                if 0 <= at < len(pulled):
                    pulled[at] = value if pulled[at] is None else pulled[at] + value

            for e in range(ext):
                value = pown[j, e, :, cols]
                if e == 0:
                    value = value * low1
                if e == ext - 1:
                    value = value * high1
                put(e - 1, value)
            for at, shift in enumerate(shifts):
                begin, end = spans[shift]
                for e in range(begin, end):
                    row = shift * rows + e - 1
                    value = precv[at, j, e, :, cols].astype(F32)
                    mask = mask_of(row)
                    put(row, value if mask is None else value * mask)
            smooth = sweep(pulled, lowest, mask_of)
            slope = [a + b for a, b in zip(smooth, extended_weights(j, lane))]
            for r in range(rows):
                own = slope[rows + r]
                grad[j, r, :, cols] = own
                square = square + own * own
            pieces.append(sweep(slope, -rows, mask_of))
        map_chunk(j, smooth_to_lhs(pieces))
        return square

    square = lax.fori_loop(0, chunks, second_forward, jnp.zeros((mem, LANES), F32))
    total_square = jnp.sum(jnp.sum(square, axis=0, keepdims=True), axis=1, keepdims=True)
    hsend[1, scalar_row : scalar_row + 1, :] = jnp.broadcast_to(total_square, (1, slots))
    observe(1, None)

    state = gathered(1)
    curve = jnp.zeros((1, slots), F32)
    for k in range(members):
        here = state[k : k + 1]
        curve = curve + fields[k][3:4] * here * here
    curve = jnp.sum(curve, axis=1, keepdims=True)
    norm = state[scalar_row : scalar_row + 1, 0:LANES]
    ids = lax.broadcasted_iota(jnp.int32, (8, LANES), 0)
    ssend[...] = jnp.where(
        ids == 0, jnp.broadcast_to(norm, (8, LANES)), jnp.broadcast_to(curve, (8, LANES))
    )

    def scalar_copy(d):
        to = lax.rem(t + d, tiles)
        return remote(ssend, srecv.at[t], s_send.at[d], s_recv.at[d], (m, to))

    for d in range(1, tiles):
        scalar_copy(d).start()
    srecv[t] = ssend[...]
    for which in range(2):
        frecv[which, m] = part[which, m]
        for d in range(1, members):
            part_copy(which, d).wait_recv()
    increment = frecv[0, 0]
    image = frecv[1, 0]
    for k in range(1, members):
        increment = increment + frecv[0, k]
        image = image + frecv[1, k]
    for d in range(1, tiles):
        scalar_copy(d).wait_recv()
    sums = srecv[0]
    for k in range(1, tiles):
        sums = sums + srecv[k]
    norm = sums[0:1, 0:1]
    step = norm / (norm + sums[1:2, 0:1])
    outi_ref[...] = increment - step * image
    step_row = jnp.broadcast_to(step, (mem, width))

    def write(j, carry):
        for r in range(rows):
            outw_ref[j, r] = w_ref[j, r] - step_row * grad[j, r]
        return carry

    lax.fori_loop(0, chunks, write, 0)

    for d in range(1, tiles):
        first_obs(d).wait_send()
        scalar_copy(d).wait_send()
    for d in range(1, members):
        second_obs(d).wait_send()
        for which in range(2):
            h_copy(which, d).wait_send()
            part_copy(which, d).wait_send()

    def drain(j, carry):
        for side in range(2):

            @pl.when(has_target(1 - 2 * side))
            def _():
                halo_copy(side, j).wait_send()

        for at, shift in enumerate(shifts):

            @pl.when(has_target(-shift))
            def _():
                pulled_copy(at, j).wait_send()

        return carry

    lax.fori_loop(0, chunks, drain, 0)


def shards(
    perturb,
    weights,
    column_map,
    background,
    stencil_index,
    row_fraction,
    column_fraction,
    block_lengths,
    obs_value,
    obs_error,
    instrument_gain,
):
    members = lax.axis_size("member")
    tiles = lax.axis_size("tile")
    fine_rows, region = background.shape
    mem, rows, coarse_cols = weights.shape
    fine_cols = column_map.shape[1]
    _, batches, owners, cap = stencil_index.shape
    slots = batches * cap
    chunks = coarse_cols // BLOCK
    ext = rows + 2
    assert rows == KSM + 1 and owners == members and members * cap <= LANES

    def by_owner(values):
        return jnp.transpose(values[0], (1, 0, 2)).reshape(owners, slots)

    index = by_owner(stencil_index)
    live = lax.broadcasted_iota(jnp.int32, (owners, batches, cap), 2) < block_lengths[0].T[..., None]
    rows_of = [
        (index // region).astype(F32),
        (index % region).astype(F32),
        by_owner(row_fraction),
        by_owner(column_fraction),
        live.astype(F32).reshape(owners, slots),
    ]
    obs = jnp.pad(jnp.stack(rows_of, axis=1), ((0, 0), (0, 3), (0, 0)))

    def by_tile(values):
        arranged = jnp.transpose(values.reshape(members, tiles, cap), (1, 0, 2))
        return jnp.pad(
            arranged.reshape(tiles, members * cap), ((0, 0), (0, LANES - members * cap))
        )

    pay = jnp.stack(
        [
            by_tile(obs_value[0]),
            by_tile(obs_error[0]),
            jnp.broadcast_to(instrument_gain[0], (tiles, LANES)),
        ],
        axis=1,
    )
    pay = jnp.pad(pay, ((0, 0), (0, 5), (0, 0)))
    w_rows = jnp.transpose(weights.reshape(mem, rows, chunks, BLOCK), (2, 1, 0, 3))
    per_rows = jnp.transpose(perturb, (1, 0, 2))

    lines = (members + 7) // 8 * 8 + 8
    vmem = pl.BlockSpec(memory_space=pltpu.VMEM)
    hbm = pl.BlockSpec(memory_space=pl.ANY)
    dma = pltpu.SemaphoreType.DMA
    out_w, increment = pl.pallas_call(
        functools.partial(kernel, members, tiles),
        out_shape=(
            jax.ShapeDtypeStruct(w_rows.shape, F32),
            jax.ShapeDtypeStruct(background.shape, F32),
        ),
        in_specs=[vmem, vmem, vmem, vmem, hbm, hbm],
        out_specs=(vmem, vmem),
        scratch_shapes=[
            pltpu.VMEM(column_map.shape, BF16),
            pltpu.VMEM(per_rows.shape, BF16),
            pltpu.VMEM((members, region, 2 * slots), BF16),
            pltpu.VMEM((members, fine_rows, slots), F32),
            pltpu.VMEM((members, 8, slots), F32),
            pltpu.VMEM((members, tiles, 8, LANES), F32),
            pltpu.VMEM(w_rows.shape, BF16),
            pltpu.VMEM((2,) + w_rows.shape, BF16),
            pltpu.VMEM((ext * mem, fine_cols), F32),
            pltpu.VMEM((fine_rows, fine_cols), F32),
            pltpu.VMEM((2, members, fine_rows, region), F32),
            pltpu.VMEM((2, members, fine_rows, region), F32),
            pltpu.VMEM((2, lines, slots), F32),
            pltpu.VMEM((2, members, lines, slots), F32),
            pltpu.VMEM((8, LANES), F32),
            pltpu.VMEM((tiles, 8, LANES), F32),
            pltpu.VMEM((fine_rows, fine_cols), F32),
            pltpu.VMEM((ext * mem, fine_cols), BF16),
            pltpu.VMEM((chunks, ext, mem, BLOCK), F32),
            pltpu.VMEM((chunks, ext, mem, BLOCK), BF16),
            pltpu.VMEM((4, chunks, ext, mem, BLOCK), BF16),
            pltpu.VMEM(w_rows.shape, F32),
            dma((2,)),
            dma((tiles,)),
            dma((tiles,)),
            dma((members,)),
            dma((members,)),
            dma((2, chunks)),
            dma((2, chunks)),
            dma((2, members)),
            dma((2, members)),
            dma((2, members)),
            dma((2, members)),
            dma((4, chunks)),
            dma((4, chunks)),
            dma((tiles,)),
            dma((tiles,)),
        ],
        compiler_params=pltpu.CompilerParams(
            collective_id=0, has_side_effects=True, vmem_limit_bytes=50 * 2**20
        ),
    )(pay, w_rows, obs, background, column_map, per_rows)
    analysis = jnp.transpose(out_w, (2, 1, 0, 3)).reshape(weights.shape)
    return analysis, increment


def solution(mesh):
    placed = (
        P("member", "tile", None),
        P("member", "tile", None),
        P(),
        P("tile", "member"),
        P("tile", None, None, None),
        P("tile", None, None, None),
        P("tile", None, None, None),
        P("tile", None, None),
        P(("member", "tile"), None, None),
        P(("member", "tile"), None, None),
        P(("member", "tile")),
    )
    return jax.shard_map(
        shards,
        mesh=mesh,
        in_specs=placed,
        out_specs=(P("member", "tile", None), P("tile", "member")),
        check_vma=False,
    )
```

```python
import functools

import jax
import jax.numpy as jnp
from jax import lax
from jax.experimental import pallas as pl
from jax.experimental.pallas import tpu as pltpu
from jax.sharding import PartitionSpec as P

RATIO = 4
KSM = 3
DIFFUSION = 0.45
BLOCK = 256
LANES = 128
MESH = pl.DeviceIdType.MESH
F32 = jnp.float32
BF16 = jnp.bfloat16


def sweep(rows, first, mask_of):
    for _ in range(KSM):
        first += 1
        inner = []
        for at in range(1, len(rows) - 1):
            mid = rows[at]
            new = mid + DIFFUSION * (rows[at - 1] + rows[at + 1] - 2.0 * mid)
            mask = mask_of(first + at - 1)
            inner.append(new if mask is None else new * mask)
        rows = inner
    return rows


def split_rows(values):
    high = values.astype(BF16)
    low = (values - high.astype(F32)).astype(BF16)
    return jnp.concatenate([high, low], axis=0)


def kernel(
    members,
    tiles,
    pay_ref,
    w_ref,
    obs_ref,
    bg_ref,
    map_hbm,
    per_hbm,
    outw_ref,
    outi_ref,
    cmap,
    per,
    hot,
    rowf,
    info,
    obsin,
    wsend,
    halo,
    acc,
    flat,
    part,
    frecv,
    hsend,
    hrecv,
    ssend,
    srecv,
    spread,
    edges,
    pown,
    psend,
    precv,
    grad,
    load_sem,
    o1_send,
    o1_recv,
    o2_send,
    o2_recv,
    w_send,
    w_recv,
    h_send,
    h_recv,
    f_send,
    f_recv,
    p_send,
    p_recv,
    s_send,
    s_recv,
):
    m = lax.axis_index("member")
    t = lax.axis_index("tile")
    rows, mem, coarse_cols = w_ref.shape
    width = BLOCK
    chunks = coarse_cols // width
    region = bg_ref.shape[1]
    fine_rows = bg_ref.shape[0]
    slots = rowf.shape[2]
    fine_cols = cmap.shape[1]
    ext = rows + 2
    cap = slots // (members * tiles)
    scalar_row = hsend.shape[1] - 8

    load_map = pltpu.make_async_copy(map_hbm, cmap, load_sem.at[0])
    load_per = pltpu.make_async_copy(per_hbm, per, load_sem.at[1])
    load_map.start()
    load_per.start()

    barrier = pltpu.get_barrier_semaphore()
    for d in range(1, members):
        pl.semaphore_signal(
            barrier, inc=1, device_id=(lax.rem(m + d, members), t), device_id_type=MESH
        )
    for d in range(1, tiles):
        pl.semaphore_signal(
            barrier, inc=1, device_id=(m, lax.rem(t + d, tiles)), device_id_type=MESH
        )

    for j in range(chunks):
        wsend[j] = w_ref[:, :, j * width : (j + 1) * width].astype(BF16)
    obsin[m, t] = pay_ref[t]
    pl.semaphore_wait(barrier, members + tiles - 2)

    def remote(src, dst, ssem, rsem, where):
        return pltpu.make_async_remote_copy(
            src_ref=src, dst_ref=dst, send_sem=ssem, recv_sem=rsem, device_id=where, device_id_type=MESH
        )

    def halo_copy(side, j):
        target = jnp.clip(t + 1 - 2 * side, 0, tiles - 1)
        return remote(
            wsend.at[j], halo.at[side, j], w_send.at[side, j], w_recv.at[side, j], (m, target)
        )

    def has_target(step):
        return (t + step >= 0) & (t + step < tiles)

    def first_obs(d):
        to = lax.rem(t + d, tiles)
        return remote(pay_ref.at[to], obsin.at[m, t], o1_send.at[d], o1_recv.at[d], (m, to))

    def second_obs(d):
        to = lax.rem(m + d, members)
        return remote(obsin.at[m], obsin.at[m], o2_send.at[d], o2_recv.at[d], (to, t))

    for d in range(1, tiles):
        first_obs(d).start()

    def send_halo(j, carry):
        for side in range(2):

            @pl.when(has_target(1 - 2 * side))
            def _():
                halo_copy(side, j).start()

        return carry

    lax.fori_loop(0, chunks, send_halo, 0)

    for side in range(2):

        @pl.when(jnp.logical_not(has_target(2 * side - 1)))
        def _():
            halo[side] = jnp.zeros(halo.shape[1:], halo.dtype)

    shifts = (-1, 1, -2, 2)
    for at, shift in enumerate(shifts):

        @pl.when(jnp.logical_not(has_target(shift)))
        def _():
            precv[at] = jnp.zeros(precv.shape[1:], precv.dtype)

    hsend[...] = jnp.zeros(hsend.shape, hsend.dtype)

    owner_ids = lax.broadcasted_iota(jnp.int32, (members * tiles, 8, slots), 0)
    lane_ids = lax.broadcasted_iota(jnp.int32, (members * tiles, 8, slots), 2)
    chosen = lane_ids // cap == owner_ids
    source = lax.broadcasted_iota(jnp.int32, (LANES, slots), 0)
    target = lax.broadcasted_iota(jnp.int32, (LANES, slots), 1)

    def arranged(listed, field):
        pick = jnp.where(source == field * cap + target % cap, 1.0, 0.0).astype(F32)
        wide = jnp.dot(
            listed.reshape(members * tiles * 8, LANES),
            pick,
            precision=lax.Precision.HIGHEST,
            preferred_element_type=F32,
        ).reshape(members * tiles, 8, slots)
        return jnp.sum(jnp.where(chosen, wide, 0.0), axis=0)

    listed = obs_ref[...]
    index = (arranged(listed, 0) + 0.5).astype(jnp.int32)
    info[0] = (index // region).astype(F32)
    info[1] = (index % region).astype(F32)
    info[2] = arranged(listed, 1)
    info[3] = arranged(listed, 2)
    slot_ids = lax.broadcasted_iota(jnp.int32, (8, slots), 1) % cap
    info[4] = jnp.where(slot_ids.astype(F32) < arranged(listed, 3), 1.0, 0.0)

    for k in range(members):
        row_pos, col_pos, row_frac = (info[f, k : k + 1] for f in range(3))
        col_ids = lax.broadcasted_iota(jnp.int32, (region, slots), 0).astype(F32)
        hot[k, :, 0:slots] = jnp.where(col_ids == col_pos, 1.0, 0.0).astype(BF16)
        hot[k, :, slots : 2 * slots] = jnp.where(col_ids == col_pos + 1.0, 1.0, 0.0).astype(BF16)
        row_ids = lax.broadcasted_iota(jnp.int32, (fine_rows, slots), 0).astype(F32)
        rowf[k] = jnp.where(row_ids == row_pos, 1.0 - row_frac, 0.0) + jnp.where(
            row_ids == row_pos + 1.0, row_frac, 0.0
        )

    for d in range(1, tiles):
        first_obs(d).wait_recv()
    for d in range(1, members):
        second_obs(d).start()

    low1 = jnp.where(t > 0, 1.0, 0.0).astype(F32)
    high1 = jnp.where(t < tiles - 1, 1.0, 0.0).astype(F32)
    low2 = jnp.where(t > 1, 1.0, 0.0).astype(F32)
    high2 = jnp.where(t < tiles - 2, 1.0, 0.0).astype(F32)

    def mask_of(row):
        if row < -rows:
            return low2
        if row < 0:
            return low1
        if row < rows:
            return None
        if row < 2 * rows:
            return high1
        return high2

    def extended_weights(j, at):
        cols = pl.ds(at * LANES, LANES)
        whole = pl.ds(pl.multiple_of(j * width + at * LANES, LANES), LANES)
        return (
            [halo[0, j, r, :, cols].astype(F32) for r in range(rows)]
            + [w_ref[r, :, whole] for r in range(rows)]
            + [halo[1, j, r, :, cols].astype(F32) for r in range(rows)]
        )

    def map_chunk(j, lhs):
        depth = pl.ds(pl.multiple_of(j * width, width), width)
        product = jnp.dot(lhs, cmap[depth, :], preferred_element_type=F32)

        @pl.when(j == 0)
        def _():
            acc[...] = product

        @pl.when(j > 0)
        def _():
            acc[...] += product

    def smooth_to_lhs(pieces):
        return jnp.concatenate(
            [
                jnp.concatenate([piece[r] for piece in pieces], axis=1).astype(BF16)
                for r in range(ext)
            ],
            axis=0,
        )

    def first_forward(j, carry):
        for side in range(2):

            @pl.when(has_target(2 * side - 1))
            def _():
                halo_copy(side, j).wait_recv()

        map_chunk(
            j,
            smooth_to_lhs(
                [sweep(extended_weights(j, at), -rows, mask_of) for at in range(width // LANES)]
            ),
        )
        return carry

    load_map.wait()
    load_per.wait()
    lax.fori_loop(0, chunks, first_forward, 0)

    weights_of = []
    for offset in range(RATIO):
        shift = (offset + 0.5) / RATIO - 0.5
        weights_of.append((1.0 - abs(shift), abs(shift), -1 if shift < 0 else 1))

    def member_sum(block, carry):
        cols = pl.ds(pl.multiple_of(block * LANES, LANES), LANES)
        mapped = [acc[pl.ds(i * mem, mem), cols] for i in range(ext)]
        lines = []
        for i in range(rows):
            for offset in range(RATIO):
                near, far, side = weights_of[offset]
                fine = near * mapped[i + 1] + far * mapped[i + 1 + side]
                term = fine * per[RATIO * i + offset, :, cols].astype(F32)
                lines.append(jnp.sum(term, axis=0, keepdims=True))
        flat[:, cols] = jnp.concatenate(lines, axis=0)
        return carry

    def part_copy(which, d):
        to = lax.rem(m + d, members)
        return remote(
            part.at[which, to], frecv.at[which, m], f_send.at[which, d], f_recv.at[which, d], (to, t)
        )

    def h_copy(which, d):
        to = lax.rem(m + d, members)
        return remote(
            hsend.at[which], hrecv.at[which, m], h_send.at[which, d], h_recv.at[which, d], (to, t)
        )

    def observe(which, scale):
        lax.fori_loop(0, fine_cols // LANES, member_sum, 0)
        for k in range(members):
            field = flat[:, k * region : (k + 1) * region]
            part[which, k] = field
            if which == 0:
                field = field + bg_ref[...] * jnp.where(m == k, 1.0, 0.0).astype(F32)
            found = jnp.dot(split_rows(field), hot[k], preferred_element_type=F32)
            found = found[:fine_rows] + found[fine_rows:]
            col_frac = info[3, k : k + 1]
            along = (1.0 - col_frac) * found[:, :slots] + col_frac * found[:, slots:]
            hsend[which, k : k + 1, :] = jnp.sum(along * rowf[k], axis=0, keepdims=True)
        for d in range(1, members):
            h_copy(which, d).start()
        for d in range(1, members):
            part_copy(which, d).start()

    def gathered(which):
        hrecv[which, m] = hsend[which]
        for d in range(1, members):
            h_copy(which, d).wait_recv()
        total = hrecv[which, 0]
        for k in range(1, members):
            total = total + hrecv[which, k]
        return total

    observe(0, None)

    for d in range(1, members):
        second_obs(d).wait_recv()
    listed = obsin[...].reshape(members * tiles, 8, LANES)
    value, error, gain = (arranged(listed, f) for f in range(3))
    precision = 1.0 / (error * error)

    state = gathered(0)

    here = state[0:8]
    bounded = jnp.tanh(here)
    slope = 1.0 + gain * (1.0 - bounded * bounded)
    info[5] = slope * (here + gain * bounded - value) * precision * info[4]
    info[6] = slope * slope * precision * info[4]

    for k in range(members):
        residual, col_frac = info[5, k : k + 1], info[3, k : k + 1]
        weighted = rowf[k] * residual
        both = jnp.concatenate([weighted * (1.0 - col_frac), weighted * col_frac], axis=1)
        found = lax.dot_general(
            split_rows(both), hot[k], (((1,), (1,)), ((), ())), preferred_element_type=F32
        )
        spread[:, k * region : (k + 1) * region] = found[:fine_rows] + found[fine_rows:]

    def adjoint_terms(block, carry):
        cols = pl.ds(pl.multiple_of(block * LANES, LANES), LANES)
        here = spread[:, cols]
        terms = [None] * ext

        def add(at, value):
            terms[at] = value if terms[at] is None else terms[at] + value

        for i in range(rows):
            for offset in range(RATIO):
                near, far, side = weights_of[offset]
                r = RATIO * i + offset
                layer = per[r, :, cols].astype(F32) * here[r : r + 1]
                add(i + 1, near * layer)
                add(i + 1 + side, far * layer)
        for at in range(ext):
            edges[pl.ds(at * mem, mem), cols] = terms[at].astype(BF16)
        return carry

    lax.fori_loop(0, fine_cols // LANES, adjoint_terms, 0)

    spans = {-1: (0, ext), 1: (0, ext), -2: (ext - rows, ext), 2: (0, rows)}

    def pulled_copy(at, j):
        shift = shifts[at]
        begin, end = spans[shift]
        to = jnp.clip(t - shift, 0, tiles - 1)
        return remote(
            psend.at[j, pl.ds(begin, end - begin)],
            precv.at[at, j, pl.ds(begin, end - begin)],
            p_send.at[at, j],
            p_recv.at[at, j],
            (m, to),
        )

    def pull(j, carry):
        depth = pl.ds(pl.multiple_of(j * width, width), width)
        product = lax.dot_general(
            edges[...], cmap[depth, :], (((1,), (1,)), ((), ())), preferred_element_type=F32
        ).reshape(ext, mem, width)
        pown[j] = product
        psend[j] = product.astype(BF16)
        for at, shift in enumerate(shifts):

            @pl.when(has_target(-shift))
            def _():
                pulled_copy(at, j).start()

        return carry

    lax.fori_loop(0, chunks, pull, 0)

    def second_forward(j, square):
        for at, shift in enumerate(shifts):

            @pl.when(has_target(shift))
            def _():
                pulled_copy(at, j).wait_recv()

        pieces = []
        for lane in range(width // LANES):
            cols = pl.ds(lane * LANES, LANES)
            lowest = -rows - KSM
            pulled = [None] * (rows + 2 * (rows + KSM))

            def put(row, value):
                at = row - lowest
                if 0 <= at < len(pulled):
                    pulled[at] = value if pulled[at] is None else pulled[at] + value

            for e in range(ext):
                value = pown[j, e, :, cols]
                if e == 0:
                    value = value * low1
                if e == ext - 1:
                    value = value * high1
                put(e - 1, value)
            for at, shift in enumerate(shifts):
                begin, end = spans[shift]
                for e in range(begin, end):
                    row = shift * rows + e - 1
                    value = precv[at, j, e, :, cols].astype(F32)
                    mask = mask_of(row)
                    put(row, value if mask is None else value * mask)
            smooth = sweep(pulled, lowest, mask_of)
            slope = [a + b for a, b in zip(smooth, extended_weights(j, lane))]
            for r in range(rows):
                own = slope[rows + r]
                grad[j, r, :, cols] = own
                square = square + own * own
            pieces.append(sweep(slope, -rows, mask_of))
        map_chunk(j, smooth_to_lhs(pieces))
        return square

    square = lax.fori_loop(0, chunks, second_forward, jnp.zeros((mem, LANES), F32))
    total_square = jnp.sum(jnp.sum(square, axis=0, keepdims=True), axis=1, keepdims=True)
    hsend[1, scalar_row : scalar_row + 1, :] = jnp.broadcast_to(total_square, (1, slots))
    observe(1, None)

    state = gathered(1)
    curve = jnp.zeros((1, slots), F32)
    for k in range(members):
        here = state[k : k + 1]
        curve = curve + info[6, k : k + 1] * here * here
    curve = jnp.sum(curve, axis=1, keepdims=True)
    norm = state[scalar_row : scalar_row + 1, 0:LANES]
    ids = lax.broadcasted_iota(jnp.int32, (8, LANES), 0)
    ssend[...] = jnp.where(
        ids == 0, jnp.broadcast_to(norm, (8, LANES)), jnp.broadcast_to(curve, (8, LANES))
    )

    def scalar_copy(d):
        to = lax.rem(t + d, tiles)
        return remote(ssend, srecv.at[t], s_send.at[d], s_recv.at[d], (m, to))

    for d in range(1, tiles):
        scalar_copy(d).start()
    srecv[t] = ssend[...]
    for which in range(2):
        frecv[which, m] = part[which, m]
        for d in range(1, members):
            part_copy(which, d).wait_recv()
    increment = frecv[0, 0]
    image = frecv[1, 0]
    for k in range(1, members):
        increment = increment + frecv[0, k]
        image = image + frecv[1, k]
    for d in range(1, tiles):
        scalar_copy(d).wait_recv()
    sums = srecv[0]
    for k in range(1, tiles):
        sums = sums + srecv[k]
    norm = sums[0:1, 0:1]
    step = norm / (norm + sums[1:2, 0:1])
    outi_ref[...] = increment - step * image
    step_row = jnp.broadcast_to(step, (mem, width))

    def write(j, carry):
        for r in range(rows):
            cols = pl.ds(pl.multiple_of(j * width, width), width)
            outw_ref[r, :, cols] = w_ref[r, :, cols] - step_row * grad[j, r]
        return carry

    lax.fori_loop(0, chunks, write, 0)

    for d in range(1, tiles):
        first_obs(d).wait_send()
        scalar_copy(d).wait_send()
    for d in range(1, members):
        second_obs(d).wait_send()
        for which in range(2):
            h_copy(which, d).wait_send()
            part_copy(which, d).wait_send()

    def drain(j, carry):
        for side in range(2):

            @pl.when(has_target(1 - 2 * side))
            def _():
                halo_copy(side, j).wait_send()

        for at, shift in enumerate(shifts):

            @pl.when(has_target(-shift))
            def _():
                pulled_copy(at, j).wait_send()

        return carry

    lax.fori_loop(0, chunks, drain, 0)


def shards(
    perturb,
    weights,
    column_map,
    background,
    stencil_index,
    row_fraction,
    column_fraction,
    block_lengths,
    obs_value,
    obs_error,
    instrument_gain,
):
    members = lax.axis_size("member")
    tiles = lax.axis_size("tile")
    fine_rows, region = background.shape
    mem, rows, coarse_cols = weights.shape
    fine_cols = column_map.shape[1]
    _, batches, owners, cap = stencil_index.shape
    slots = batches * cap
    chunks = coarse_cols // BLOCK
    ext = rows + 2
    assert rows == KSM + 1 and owners == members and members <= 8 and 4 * cap <= LANES

    def rows_of(parts):
        parts = jnp.concatenate(parts, axis=-1)
        return jnp.pad(
            parts, ((0, 0), (0, 8 - parts.shape[1]), (0, LANES - parts.shape[2]))
        )

    lengths = jnp.broadcast_to(block_lengths[0][..., None], stencil_index.shape[1:])
    obs = rows_of(
        [stencil_index[0].astype(F32), row_fraction[0], column_fraction[0], lengths.astype(F32)]
    )
    gain = jnp.broadcast_to(instrument_gain, obs_value.shape[1:])
    batch = jnp.concatenate([obs_value[0], obs_error[0], gain], axis=-1)
    pay = rows_of([jnp.transpose(batch.reshape(members, tiles, 3 * cap), (1, 0, 2))])
    w_rows = jnp.transpose(weights, (1, 0, 2))
    per_rows = jnp.transpose(perturb, (1, 0, 2))

    lines = (members + 7) // 8 * 8 + 8
    vmem = pl.BlockSpec(memory_space=pltpu.VMEM)
    hbm = pl.BlockSpec(memory_space=pl.ANY)
    dma = pltpu.SemaphoreType.DMA
    out_w, increment = pl.pallas_call(
        functools.partial(kernel, members, tiles),
        out_shape=(
            jax.ShapeDtypeStruct(w_rows.shape, F32),
            jax.ShapeDtypeStruct(background.shape, F32),
        ),
        in_specs=[vmem, vmem, vmem, vmem, hbm, hbm],
        out_specs=(vmem, vmem),
        scratch_shapes=[
            pltpu.VMEM(column_map.shape, BF16),
            pltpu.VMEM(per_rows.shape, BF16),
            pltpu.VMEM((members, region, 2 * slots), BF16),
            pltpu.VMEM((members, fine_rows, slots), F32),
            pltpu.VMEM((7, 8, slots), F32),
            pltpu.VMEM((members, tiles, 8, LANES), F32),
            pltpu.VMEM((chunks, rows, mem, BLOCK), BF16),
            pltpu.VMEM((2, chunks, rows, mem, BLOCK), BF16),
            pltpu.VMEM((ext * mem, fine_cols), F32),
            pltpu.VMEM((fine_rows, fine_cols), F32),
            pltpu.VMEM((2, members, fine_rows, region), F32),
            pltpu.VMEM((2, members, fine_rows, region), F32),
            pltpu.VMEM((2, lines, slots), F32),
            pltpu.VMEM((2, members, lines, slots), F32),
            pltpu.VMEM((8, LANES), F32),
            pltpu.VMEM((tiles, 8, LANES), F32),
            pltpu.VMEM((fine_rows, fine_cols), F32),
            pltpu.VMEM((ext * mem, fine_cols), BF16),
            pltpu.VMEM((chunks, ext, mem, BLOCK), F32),
            pltpu.VMEM((chunks, ext, mem, BLOCK), BF16),
            pltpu.VMEM((4, chunks, ext, mem, BLOCK), BF16),
            pltpu.VMEM((chunks, rows, mem, BLOCK), F32),
            dma((2,)),
            dma((tiles,)),
            dma((tiles,)),
            dma((members,)),
            dma((members,)),
            dma((2, chunks)),
            dma((2, chunks)),
            dma((2, members)),
            dma((2, members)),
            dma((2, members)),
            dma((2, members)),
            dma((4, chunks)),
            dma((4, chunks)),
            dma((tiles,)),
            dma((tiles,)),
        ],
        compiler_params=pltpu.CompilerParams(
            collective_id=0, has_side_effects=True, vmem_limit_bytes=50 * 2**20
        ),
    )(pay, w_rows, obs, background, column_map, per_rows)
    return jnp.transpose(out_w, (1, 0, 2)), increment


def solution(mesh):
    placed = (
        P("member", "tile", None),
        P("member", "tile", None),
        P(),
        P("tile", "member"),
        P("tile", None, None, None),
        P("tile", None, None, None),
        P("tile", None, None, None),
        P("tile", None, None),
        P(("member", "tile"), None, None),
        P(("member", "tile"), None, None),
        P(("member", "tile")),
    )
    return jax.shard_map(
        shards,
        mesh=mesh,
        in_specs=placed,
        out_specs=(P("member", "tile", None), P("tile", "member")),
        check_vma=False,
    )
```
